512 devices in a mesh: dp: 64 (over z, y_hi, core), mp: 8 (over y_lo, x).
Axes of the slice: x: 4, y: 4 (y_hi: 2, y_lo: 2; y = y_hi * 2 + y_lo), z: 16, core: 2. Of those that a mesh axis runs over, the one named last changes fastest.
Arguments:
- inputs: float32 [512, 6144], P('dp', 'mp'), may hold values from -6 to 6
- w_in: float32 [6144, 24576], P('mp', 'dp'), may hold values from -0.078125 to 0.078125
- w_out: float32 [24576, 6144], P('dp', 'mp'), may hold values from -0.0390625 to 0.0390625
- cotangent: float32 [512, 6144], P('dp', 'mp'), may hold values from -6 to 6
Outputs:
- output: float32 [512, 6144], P('dp', 'mp')
- input_grad: float32 [512, 6144], P('dp', 'mp')
- w_in_grad: float32 [6144, 24576], P('mp', 'dp')
- w_out_grad: float32 [24576, 6144], P('dp', 'mp')
The draws below stay inside these ranges and needn't reach their ends.
All inputs are finite; a program needn't handle non-finite values.
Results may differ from the reference program's by a relative error of at most 0.000088.
Values sent between devices are 32-bit elements; how exact they have to be, the bound alone decides.
No kernel may reach another device: no remote copies, remote signals or barrier semaphores. Data moves between devices by JAX's collectives and lax.ppermute only.
A program may use at most 64 MiB of HBM per device.

```python
from functools import partial
import jax
import jax.numpy as jnp
from jax import lax

D = 6144
FF = 24576
TOKENS = 512


def block_levels(rng, dims, split, least, largest):
    def one(dim, parts):
        heights = jax.random.uniform(jax.random.fold_in(jax.random.fold_in(rng, 6), dim), (parts,), jnp.float32, least / len(split), largest / len(split))
        return jnp.repeat(jnp.exp(heights), dims[dim] // parts).reshape((-1,) + (1,) * (len(dims) - dim - 1))

    gain = one(*split[0])
    for cut in split[1:]:
        gain = gain * one(*cut)
    return gain


def noise(own_key, dims, scale, reach, cuts=(), kind=jnp.bfloat16):
    array = jax.random.normal(own_key, dims, jnp.float32) * scale
    if len(cuts) > 0:
        array = block_levels(own_key, dims, cuts, -0.22, 0.18) * array
    return jnp.clip(array, min=-reach, max=reach).astype(kind)


def setup_inputs(seed: int = 0) -> dict:
    key_list = jax.random.split(jax.random.key(seed), 5)
    inputs = noise(key_list[0], (TOKENS, D), 1.0, 6.0, ((0, 64), (1, 8)), jnp.float32)
    w_in = noise(key_list[1], (D, FF), D ** -0.5, 0.078125, ((0, 8), (1, 64)), jnp.float32)
    w_out = noise(key_list[2], (FF, D), FF ** -0.5, 0.0390625, ((0, 64), (1, 8)), jnp.float32)
    cotangent = noise(key_list[3], (TOKENS, D), 1.0, 6.0, ((0, 64), (1, 8)), jnp.float32)
    return dict(inputs=inputs, w_in=w_in, w_out=w_out, cotangent=cotangent)


def reference(inputs, w_in, w_out, cotangent):
    highest = lax.Precision.HIGHEST
    gelu_fn = partial(jax.nn.gelu, approximate=True)
    hidden = jnp.dot(inputs, w_in, precision=highest, preferred_element_type=jnp.float32)
    activated, gelu_back = jax.vjp(gelu_fn, hidden)
    output = jnp.dot(activated, w_out, precision=highest, preferred_element_type=jnp.float32)
    act_grad = jnp.einsum('td,fd->tf', cotangent, w_out, precision=highest)
    hid_grad = gelu_back(act_grad)[0]
    w_out_grad = jnp.einsum('tf,td->fd', activated, cotangent, precision=highest)
    w_in_grad = jnp.einsum('td,tf->df', inputs, hid_grad, precision=highest)
    input_grad = jnp.einsum('tf,df->td', hid_grad, w_in, precision=highest)
    return (output, input_grad, w_in_grad, w_out_grad)
```

```python
from functools import partial

import jax
import jax.numpy as jnp
from jax import lax
from jax.sharding import PartitionSpec as P

NZ, NY, NC = 16, 2, 2
Z_GROUPS = [[z * NY * NC + q for z in range(NZ)] for q in range(NY * NC)]
CORE_SWAP = [(d, d ^ 1) for d in range(NZ * NY * NC)]
Y_SWAP = [(d, d ^ 2) for d in range(NZ * NY * NC)]

dot = partial(lax.dot_general, precision=lax.Precision.HIGH, preferred_element_type=jnp.float32)


def mm(a, b):
    return dot(a, b, (((1,), (0,)), ((), ())))


def mm_nt(a, b):
    return dot(a, b, (((1,), (1,)), ((), ())))


def mm_tn(a, b):
    return dot(a, b, (((0,), (0,)), ((), ())))


def spread(part):
    mine = jnp.concatenate([part, lax.ppermute(part, "dp", Y_SWAP)], axis=0)
    return jnp.concatenate([mine, lax.ppermute(mine, "dp", CORE_SWAP)], axis=0)


def sum_mp(term):
    n = lax.axis_size("mp")
    got = lax.all_to_all(term, "mp", 0, 0, tiled=True)
    return got.reshape(n, term.shape[0] // n, term.shape[1]).sum(0)


def gather_mp(part):
    copies = jnp.tile(part, (lax.axis_size("mp"), 1))
    return lax.all_to_all(copies, "mp", 0, 0, tiled=True)


def scatter_dp(term):
    half = term.shape[0] // 2
    term = term[:half] + lax.ppermute(term[half:], "dp", CORE_SWAP)
    half //= 2
    term = term[:half] + lax.ppermute(term[half:], "dp", Y_SWAP)
    got = lax.all_to_all(term, "dp", 0, 0, tiled=True, axis_index_groups=Z_GROUPS)
    return got.reshape(NZ, half // NZ, term.shape[1]).sum(0)


def shards(inputs, w_in, w_out, cotangent):
    gelu_fn = partial(jax.nn.gelu, approximate=True)
    rows, width = inputs.shape
    both = jnp.concatenate([inputs, cotangent], axis=0)
    ring = lax.all_gather(both, "dp", axis=0, axis_index_groups=Z_GROUPS)
    tokens = spread(ring[:, :rows].reshape(NZ * rows, width))
    hidden = sum_mp(mm(tokens, w_in))
    grads = spread(ring[:, rows:].reshape(NZ * rows, width))
    act_grad = sum_mp(mm_nt(grads, w_out))
    activated, gelu_back = jax.vjp(gelu_fn, hidden)
    hid_grad = gelu_back(act_grad)[0]
    activated = gather_mp(activated)
    hid_grad = gather_mp(hid_grad)
    output = scatter_dp(mm(activated, w_out))
    input_grad = scatter_dp(mm_nt(hid_grad, w_in))
    w_out_grad = mm_tn(activated, grads)
    w_in_grad = mm_tn(tokens, hid_grad)
    return (output, input_grad, w_in_grad, w_out_grad)


def solution(mesh):
    placed = (P("dp", "mp"), P("mp", "dp"), P("dp", "mp"), P("dp", "mp"))
    return jax.shard_map(
        shards,
        mesh=mesh,
        in_specs=placed,
        out_specs=(P("dp", "mp"), P("dp", "mp"), P("mp", "dp"), P("dp", "mp")),
        check_vma=False,
    )
```

```python
from functools import partial

import jax
import jax.numpy as jnp
from jax import lax
from jax.sharding import PartitionSpec as P

NZ, NY, NC = 16, 2, 2
NQ = NY * NC
Z_GROUPS = [[z * NQ + q for z in range(NZ)] for q in range(NQ)]
CORE_SWAP = [(d, d ^ 1) for d in range(NZ * NQ)]
Y_SWAP = [(d, d ^ NC) for d in range(NZ * NQ)]
BOTH_SWAP = [(d, d ^ (NC + 1)) for d in range(NZ * NQ)]

dot = partial(lax.dot_general, precision=lax.Precision.HIGH, preferred_element_type=jnp.float32)


def mm(a, b):
    return dot(a, b, (((1,), (0,)), ((), ())))


def mm_nt(a, b):
    return dot(a, b, (((1,), (1,)), ((), ())))


def mm_tn(a, b):
    return dot(a, b, (((0,), (0,)), ((), ())))


def swap(x, pairs):
    return lax.ppermute(x, "dp", pairs)


def after(x, y):
    return lax.optimization_barrier((x, y))[0]


def sum_mp(term):
    n = lax.axis_size("mp")
    got = lax.all_to_all(term, "mp", 0, 0, tiled=True)
    return got.reshape(n, term.shape[0] // n, term.shape[1]).sum(0)


def gather_mp(part):
    copies = jnp.tile(part, (lax.axis_size("mp"), 1))
    return lax.all_to_all(copies, "mp", 0, 0, tiled=True)


def shards(inputs, w_in, w_out, cotangent):
    gelu_fn = partial(jax.nn.gelu, approximate=True)
    rows, width = inputs.shape
    ff = w_in.shape[1]
    n = NZ * rows

    w_in_y = swap(w_in, Y_SWAP)
    w_out_y = swap(w_out, Y_SWAP)
    w_in_c = swap(w_in, CORE_SWAP)
    w_out_c = swap(w_out, CORE_SWAP)
    both = jnp.concatenate([inputs, cotangent], axis=0)
    ring = lax.all_gather(both, "dp", axis=0, axis_index_groups=Z_GROUPS)
    w_ins = [w_in, w_in_c, w_in_y, swap(after(w_in_y, ring), CORE_SWAP)]
    w_outs = [w_out, w_out_c, w_out_y, swap(after(w_out_y, ring), CORE_SWAP)]

    tok = ring[:, :rows].reshape(n, width)
    grd = ring[:, rows:].reshape(n, width)

    terms = jnp.concatenate([mm(tok, w) for w in w_ins] + [mm_nt(grd, w) for w in w_outs], axis=1)
    sums = sum_mp(terms)
    activated, gelu_back = jax.vjp(gelu_fn, sums[:, : NQ * ff])
    hid_grad = gelu_back(sums[:, NQ * ff :])[0]
    full = gather_mp(jnp.concatenate([activated, hid_grad], axis=1))
    act, hg = full[:, : NQ * ff], full[:, NQ * ff :]
    out_term = mm(act, jnp.concatenate(w_outs, axis=0))
    in_term = mm_nt(hg, jnp.concatenate(w_ins, axis=1))
    terms = jnp.concatenate([out_term.reshape(NZ, rows, width), in_term.reshape(NZ, rows, width)], axis=1)
    got = lax.all_to_all(terms, "dp", 0, 0, tiled=True, axis_index_groups=Z_GROUPS).sum(0)
    output, input_grad = got[:rows], got[rows:]

    tg = jnp.concatenate([tok, grd], axis=0)
    tg_y = swap(after(tg, full), Y_SWAP)
    part = [jnp.concatenate([act[:, k * ff : (k + 1) * ff], hg[:, k * ff : (k + 1) * ff]], axis=1) for k in range(NQ)]
    part_y = swap(part[2], Y_SWAP)
    part_yc = swap(part[3], BOTH_SWAP)
    part_c = swap(part[1], CORE_SWAP)
    tg_c = swap(tg, CORE_SWAP)
    tg_yc = swap(tg_y, CORE_SWAP)

    def grads(tgs, parts):
        t = jnp.concatenate([x[:n] for x in tgs], axis=0)
        c = jnp.concatenate([x[n:] for x in tgs], axis=0)
        p = jnp.concatenate(parts, axis=0)
        return mm_tn(t, p[:, ff:]), mm_tn(p[:, :ff], c)

    near, far = grads([tg, tg_c], [part[0], part_c]), grads([tg_y, tg_yc], [part_y, part_yc])
    w_in_grad = near[0] + far[0]
    w_out_grad = near[1] + far[1]
    return (output, input_grad, w_in_grad, w_out_grad)


def solution(mesh):
    placed = (P("dp", "mp"), P("mp", "dp"), P("dp", "mp"), P("dp", "mp"))
    return jax.shard_map(
        shards,
        mesh=mesh,
        in_specs=placed,
        out_specs=(P("dp", "mp"), P("dp", "mp"), P("mp", "dp"), P("dp", "mp")),
        check_vma=False,
    )
```

```python
from functools import partial

import jax
import jax.numpy as jnp
from jax import lax
from jax.sharding import PartitionSpec as P

NZ, NY, NC = 16, 2, 2
NQ = NY * NC
Z_GROUPS = [[z * NQ + q for z in range(NZ)] for q in range(NQ)]
CORE_SWAP = [(d, d ^ 1) for d in range(NZ * NQ)]
Y_SWAP = [(d, d ^ NC) for d in range(NZ * NQ)]
BOTH_SWAP = [(d, d ^ (NC + 1)) for d in range(NZ * NQ)]

dot = partial(lax.dot_general, precision=lax.Precision.HIGH, preferred_element_type=jnp.float32)


def mm(a, b):
    return dot(a, b, (((1,), (0,)), ((), ())))


def mm_nt(a, b):
    return dot(a, b, (((1,), (1,)), ((), ())))


def mm_tn(a, b):
    return dot(a, b, (((0,), (0,)), ((), ())))


def swap(x, pairs):
    return lax.ppermute(x, "dp", pairs)


def after(x, y):
    return lax.optimization_barrier((x, y))[0]


def sum_mp(term):
    n = lax.axis_size("mp")
    got = lax.all_to_all(term, "mp", 0, 0, tiled=True)
    return got.reshape(n, term.shape[0] // n, term.shape[1]).sum(0)


def gather_mp(part):
    copies = jnp.tile(part, (lax.axis_size("mp"), 1))
    return lax.all_to_all(copies, "mp", 0, 0, tiled=True)


def shards(inputs, w_in, w_out, cotangent):
    gelu_fn = partial(jax.nn.gelu, approximate=True)
    rows, width = inputs.shape
    ff = w_in.shape[1]
    n = NZ * rows

    w_in_y = swap(w_in, Y_SWAP)
    w_out_y = swap(w_out, Y_SWAP)
    w_in_c = swap(w_in, CORE_SWAP)
    w_out_c = swap(w_out, CORE_SWAP)
    both = jnp.concatenate([inputs, cotangent], axis=0)
    ring = lax.all_gather(both, "dp", axis=0, axis_index_groups=Z_GROUPS)
    w_ins = [w_in, w_in_c, w_in_y, swap(after(w_in_y, ring), CORE_SWAP)]
    w_outs = [w_out, w_out_c, w_out_y, swap(after(w_out_y, ring), CORE_SWAP)]

    tok = ring[:, :rows].reshape(n, width)
    grd = ring[:, rows:].reshape(n, width)

    terms = jnp.concatenate([mm(tok, w) for w in w_ins] + [mm_nt(grd, w) for w in w_outs], axis=1)
    sums = sum_mp(terms)
    activated, gelu_back = jax.vjp(gelu_fn, sums[:, : NQ * ff])
    hid_grad = gelu_back(sums[:, NQ * ff :])[0]
    full = gather_mp(jnp.concatenate([activated, hid_grad], axis=1))
    act, hg = full[:, : NQ * ff], full[:, NQ * ff :]
    out_term = mm(act, jnp.concatenate(w_outs, axis=0))
    in_term = mm_nt(hg, jnp.concatenate(w_ins, axis=1))
    terms = jnp.concatenate([out_term.reshape(NZ, rows, width), in_term.reshape(NZ, rows, width)], axis=1)
    got = lax.all_to_all(terms, "dp", 0, 0, tiled=True, axis_index_groups=Z_GROUPS).sum(0)
    output, input_grad = got[:rows], got[rows:]

    tg = jnp.concatenate([tok, grd], axis=0)
    tg_c = swap(after(tg, sums), CORE_SWAP)
    tg_y = swap(after(tg, tg_c), Y_SWAP)
    part = [jnp.concatenate([act[:, k * ff : (k + 1) * ff], hg[:, k * ff : (k + 1) * ff]], axis=1) for k in range(NQ)]
    part_y = swap(part[2], Y_SWAP)
    part_yc = swap(part[3], BOTH_SWAP)
    part_c = swap(part[1], CORE_SWAP)
    tg_yc = swap(tg_y, CORE_SWAP)

    def grads(tgs, parts):
        t = jnp.concatenate([x[:n] for x in tgs], axis=0)
        c = jnp.concatenate([x[n:] for x in tgs], axis=0)
        p = jnp.concatenate(parts, axis=0)
        return mm_tn(t, p[:, ff:]), mm_tn(p[:, :ff], c)

    near, far = grads([tg, tg_c], [part[0], part_c]), grads([tg_y, tg_yc], [part_y, part_yc])
    w_in_grad = near[0] + far[0]
    w_out_grad = near[1] + far[1]
    return (output, input_grad, w_in_grad, w_out_grad)


def solution(mesh):
    placed = (P("dp", "mp"), P("mp", "dp"), P("dp", "mp"), P("dp", "mp"))
    return jax.shard_map(
        shards,
        mesh=mesh,
        in_specs=placed,
        out_specs=(P("dp", "mp"), P("dp", "mp"), P("mp", "dp"), P("dp", "mp")),
        check_vma=False,
    )
```

```python
from functools import partial

import jax
import jax.numpy as jnp
from jax import lax
from jax.sharding import PartitionSpec as P

NZ, NY, NC = 16, 2, 2
NQ = NY * NC
Z_GROUPS = [[z * NQ + q for z in range(NZ)] for q in range(NQ)]
CORE_SWAP = [(d, d ^ 1) for d in range(NZ * NQ)]
Y_SWAP = [(d, d ^ NC) for d in range(NZ * NQ)]
BOTH_SWAP = [(d, d ^ (NC + 1)) for d in range(NZ * NQ)]

dot = partial(lax.dot_general, precision=lax.Precision.HIGH, preferred_element_type=jnp.float32)


def mm(a, b):
    return dot(a, b, (((1,), (0,)), ((), ())))


def mm_nt(a, b):
    return dot(a, b, (((1,), (1,)), ((), ())))


def mm_tn(a, b):
    return dot(a, b, (((0,), (0,)), ((), ())))


def swap(x, pairs):
    return lax.ppermute(x, "dp", pairs)


def after(x, y):
    return lax.optimization_barrier((x, y))[0]


def sum_mp(term):
    n = lax.axis_size("mp")
    got = lax.all_to_all(term, "mp", 0, 0, tiled=True)
    return got.reshape(n, term.shape[0] // n, term.shape[1]).sum(0)


def gather_mp(part):
    copies = jnp.tile(part, (lax.axis_size("mp"), 1))
    return lax.all_to_all(copies, "mp", 0, 0, tiled=True)


def shards(inputs, w_in, w_out, cotangent):
    gelu_fn = partial(jax.nn.gelu, approximate=True)
    rows, width = inputs.shape
    ff = w_in.shape[1]
    n = NZ * rows

    w_in_y = swap(w_in, Y_SWAP)
    w_out_y = swap(w_out, Y_SWAP)
    w_in_c = swap(w_in, CORE_SWAP)
    w_out_c = swap(w_out, CORE_SWAP)
    both = jnp.concatenate([inputs, cotangent], axis=0)
    ring = lax.all_gather(both, "dp", axis=0, axis_index_groups=Z_GROUPS)
    w_ins = [w_in, w_in_c, w_in_y, swap(after(w_in_y, ring), CORE_SWAP)]
    tok = ring[:, :rows].reshape(n, width)
    grd = ring[:, rows:].reshape(n, width)

    blocks = [mm(tok, w_in), mm(tok, w_in_c), mm_nt(grd, w_out), mm_nt(grd, w_out_c)]
    w_outs = [w_out, w_out_c, w_out_y, swap(after(w_out_y, blocks[:2]), CORE_SWAP)]
    terms = blocks[:2] + [mm(tok, w) for w in w_ins[2:]] + blocks[2:] + [mm_nt(grd, w) for w in w_outs[2:]]
    terms = jnp.concatenate(terms, axis=1)
    sums = sum_mp(terms)
    activated, gelu_back = jax.vjp(gelu_fn, sums[:, : NQ * ff])
    hid_grad = gelu_back(sums[:, NQ * ff :])[0]
    full = gather_mp(jnp.concatenate([activated, hid_grad], axis=1))
    act, hg = full[:, : NQ * ff], full[:, NQ * ff :]
    out_term = mm(act, jnp.concatenate(w_outs, axis=0))
    in_term = mm_nt(hg, jnp.concatenate(w_ins, axis=1))
    terms = jnp.concatenate([out_term.reshape(NZ, rows, width), in_term.reshape(NZ, rows, width)], axis=1)
    got = lax.all_to_all(terms, "dp", 0, 0, tiled=True, axis_index_groups=Z_GROUPS).sum(0)
    output, input_grad = got[:rows], got[rows:]

    tg = jnp.concatenate([tok, grd], axis=0)
    tg_c = swap(after(tg, sums), CORE_SWAP)
    tg_y = swap(after(tg, tg_c), Y_SWAP)
    part = [jnp.concatenate([act[:, k * ff : (k + 1) * ff], hg[:, k * ff : (k + 1) * ff]], axis=1) for k in range(NQ)]
    part_y = swap(part[2], Y_SWAP)
    part_yc = swap(part[3], BOTH_SWAP)
    part_c = swap(part[1], CORE_SWAP)
    tg_yc = swap(tg_y, CORE_SWAP)

    def grads(tgs, parts):
        t = jnp.concatenate([x[:n] for x in tgs], axis=0)
        c = jnp.concatenate([x[n:] for x in tgs], axis=0)
        p = jnp.concatenate(parts, axis=0)
        return mm_tn(t, p[:, ff:]), mm_tn(p[:, :ff], c)

    near, far = grads([tg, tg_c], [part[0], part_c]), grads([tg_y, tg_yc], [part_y, part_yc])
    w_in_grad = near[0] + far[0]
    w_out_grad = near[1] + far[1]
    return (output, input_grad, w_in_grad, w_out_grad)


def solution(mesh):
    placed = (P("dp", "mp"), P("mp", "dp"), P("dp", "mp"), P("dp", "mp"))
    return jax.shard_map(
        shards,
        mesh=mesh,
        in_specs=placed,
        out_specs=(P("dp", "mp"), P("dp", "mp"), P("mp", "dp"), P("dp", "mp")),
        check_vma=False,
    )
```

```python
from functools import partial

import jax
import jax.numpy as jnp
from jax import lax
from jax.sharding import PartitionSpec as P

NZ, NY, NC = 16, 2, 2
NQ = NY * NC
Z_GROUPS = [[z * NQ + q for z in range(NZ)] for q in range(NQ)]
CORE_SWAP = [(d, d ^ 1) for d in range(NZ * NQ)]
Y_SWAP = [(d, d ^ NC) for d in range(NZ * NQ)]
BOTH_SWAP = [(d, d ^ (NC + 1)) for d in range(NZ * NQ)]

dot = partial(lax.dot_general, precision=lax.Precision.HIGH, preferred_element_type=jnp.float32)


def mm(a, b):
    return dot(a, b, (((1,), (0,)), ((), ())))


def mm_nt(a, b):
    return dot(a, b, (((1,), (1,)), ((), ())))


def mm_tn(a, b):
    return dot(a, b, (((0,), (0,)), ((), ())))


def swap(x, pairs):
    return lax.ppermute(x, "dp", pairs)


def after(x, y):
    return lax.optimization_barrier((x, y))[0]


def sum_mp(term):
    n = lax.axis_size("mp")
    got = lax.all_to_all(term, "mp", 0, 0, tiled=True)
    return got.reshape(n, term.shape[0] // n, term.shape[1]).sum(0)


def gather_mp(part):
    copies = jnp.tile(part, (lax.axis_size("mp"), 1))
    return lax.all_to_all(copies, "mp", 0, 0, tiled=True)


def shards(inputs, w_in, w_out, cotangent):
    gelu_fn = partial(jax.nn.gelu, approximate=True)
    rows, width = inputs.shape
    ff = w_in.shape[1]
    n = NZ * rows

    w_in_y = swap(w_in, Y_SWAP)
    w_out_y = swap(w_out, Y_SWAP)
    w_in_c = swap(w_in, CORE_SWAP)
    w_out_c = swap(w_out, CORE_SWAP)
    both = jnp.concatenate([inputs, cotangent], axis=0)
    ring = lax.all_gather(both, "dp", axis=0, axis_index_groups=Z_GROUPS)
    w_ins = [w_in, w_in_c, w_in_y, swap(after(w_in_y, ring), CORE_SWAP)]
    tok = ring[:, :rows].reshape(n, width)
    grd = ring[:, rows:].reshape(n, width)

    blocks = [mm(tok, w_in), mm(tok, w_in_c), mm_nt(grd, w_out), mm_nt(grd, w_out_c)]
    w_outs = [w_out, w_out_c, w_out_y, swap(after(w_out_y, blocks[:2]), CORE_SWAP)]
    terms = blocks[:2] + [mm(tok, w) for w in w_ins[2:]] + blocks[2:] + [mm_nt(grd, w) for w in w_outs[2:]]
    terms = jnp.concatenate(terms, axis=1)
    sums = sum_mp(terms)
    activated, gelu_back = jax.vjp(gelu_fn, sums[:, : NQ * ff])
    hid_grad = gelu_back(sums[:, NQ * ff :])[0]
    full = gather_mp(jnp.concatenate([activated, hid_grad], axis=1))
    act, hg = full[:, : NQ * ff], full[:, NQ * ff :]
    out_term = mm(act, jnp.concatenate(w_outs, axis=0))
    in_term = mm_nt(hg, jnp.concatenate(w_ins, axis=1))
    terms = jnp.concatenate([out_term.reshape(NZ, rows, width), in_term.reshape(NZ, rows, width)], axis=1)
    got = lax.all_to_all(terms, "dp", 0, 0, tiled=True, axis_index_groups=Z_GROUPS).sum(0)
    output, input_grad = got[:rows], got[rows:]

    tg = jnp.concatenate([tok, grd], axis=0)
    tg_c = swap(after(tg, sums), CORE_SWAP)
    tg_y = swap(after(tg, tg_c), Y_SWAP)
    act_, hg_ = after((act, hg), terms)
    part = [jnp.concatenate([act_[:, k * ff : (k + 1) * ff], hg_[:, k * ff : (k + 1) * ff]], axis=1) for k in range(NQ)]
    part_y = swap(part[2], Y_SWAP)
    part_yc = swap(part[3], BOTH_SWAP)
    part_c = swap(part[1], CORE_SWAP)
    tg_yc = swap(tg_y, CORE_SWAP)

    def grads(tgs, parts):
        t = jnp.concatenate([x[:n] for x in tgs], axis=0)
        c = jnp.concatenate([x[n:] for x in tgs], axis=0)
        p = jnp.concatenate(parts, axis=0)
        return mm_tn(t, p[:, ff:]), mm_tn(p[:, :ff], c)

    near, far = grads([tg, tg_c], [part[0], part_c]), grads([tg_y, tg_yc], [part_y, part_yc])
    w_in_grad = near[0] + far[0]
    w_out_grad = near[1] + far[1]
    return (output, input_grad, w_in_grad, w_out_grad)


def solution(mesh):
    placed = (P("dp", "mp"), P("mp", "dp"), P("dp", "mp"), P("dp", "mp"))
    return jax.shard_map(
        shards,
        mesh=mesh,
        in_specs=placed,
        out_specs=(P("dp", "mp"), P("dp", "mp"), P("mp", "dp"), P("dp", "mp")),
        check_vma=False,
    )
```
